512 devices in a mesh: dp: 16 (over z, core), pp: 16 (over x_hi, y), tp: 2 (over x_lo).
Axes of the slice: x: 4 (x_hi: 2, x_lo: 2; x = x_hi * 2 + x_lo), y: 8, z: 8, core: 2. Of those that a mesh axis runs over, the one named last changes fastest.
Arguments:
- activations: bfloat16 [16, 4096, 4096], P('pp', 'dp', 'tp'), may hold values from -6 to 6
- key_grads: bfloat16 [16, 4096, 512], P('pp', 'dp', 'tp'), may hold values from -6 to 6
- key_weight: bfloat16 [16, 4096, 512], P('pp', 'dp', 'tp'), may hold values from -0.25 to 0.25
- error_buf: bfloat16 [16, 16, 4096, 512], P('pp', 'dp', None, 'tp'), may hold values from -96 to 96
- q_prev: float32 [16, 512, 64], P('pp', 'tp'), may hold values from -0.25 to 0.25
Outputs:
- grad_prev: bfloat16 [16, 4096, 4096], P('pp', 'dp', 'tp')
- q_new: float32 [16, 512, 64], P('pp', 'tp')
The draws below stay inside these ranges and needn't reach their ends.
All inputs are finite; a program needn't handle non-finite values.
Results may differ from the reference program's by a relative error of at most 0.015.
Values may be sent and summed in bfloat16 or wider, within the bound.
No kernel may reach another device: no remote copies, remote signals or barrier semaphores. Data moves between devices by JAX's collectives and lax.ppermute only.
A program may use at most 64 MiB of HBM per device.

```python
import jax
import jax.numpy as jnp
from jax import lax

D = 4096
KVW = 512
R = 64
TOK_DEV = 256
TOKENS = 4096
N_DP = 16
N_PP = 16
N_TP = 2


def levels(stream_key, shape, shards, smallest, high):
    gain, own = 1.0, jax.random.fold_in(stream_key, 6)
    for position, blocks in shards:
        heights = jnp.exp(jax.random.uniform(jax.random.fold_in(own, position), (blocks,), jnp.float32, smallest / len(shards), high / len(shards)))
        gain = gain * jnp.repeat(heights, shape[position] // blocks).reshape([-1 if axis == position else 1 for axis in range(len(shape))])
    return gain


def noise(rng, extent, deviation, reach, pieces=(), kind=jnp.bfloat16):
    array = jax.random.normal(rng, extent, jnp.float32) * deviation
    if len(pieces) > 0:
        array = levels(rng, extent, pieces, -0.22, 0.18) * array
    return jnp.clip(array, min=-reach, max=reach).astype(kind)


def setup_inputs(seed: int = 0) -> dict:
    key_list = jax.random.split(jax.random.key(seed), 6)
    return {
        "activations": noise(key_list[0], (N_PP, TOKENS, D), 1.0, 6.0, ((0, 16), (1, 16), (2, 2))),
        "key_grads": noise(key_list[1], (N_PP, TOKENS, KVW), 1.0, 6.0, ((0, 16), (1, 16), (2, 2))),
        "key_weight": noise(key_list[2], (N_PP, D, KVW), KVW ** -0.5, 0.25, ((0, 16), (1, 16), (2, 2))),
        "error_buf": noise(key_list[3], (N_PP, N_DP, D, KVW), 16.0, 96.0, ((0, 16), (1, 16), (3, 2))),
        "q_prev": noise(key_list[4], (N_PP, KVW, R), KVW ** -0.5, 0.25, ((0, 16), (1, 2)), jnp.float32),
    }


HIGHEST = lax.Precision.HIGHEST

def section_gradient(operands):
    grads_section, weight_section = operands
    block_width = KVW // N_TP
    total = jnp.zeros((TOKENS, D), jnp.float32)
    for which_block in range(N_TP):
        first_col = which_block * block_width
        term = jnp.dot(grads_section[:, first_col:first_col + block_width].astype(jnp.float32), weight_section[:, first_col:first_col + block_width].T.astype(jnp.float32), preferred_element_type=jnp.float32).astype(jnp.bfloat16)
        term = lax.optimization_barrier(term)
        total = total + term.astype(jnp.float32)
    return total.astype(jnp.bfloat16)

def section_factors(operands):
    inputs_section, grads_section, error_section, coeffs_prev = operands
    inputs_groups = inputs_section.reshape(N_DP, TOK_DEV, D)
    grads_groups = grads_section.reshape(N_DP, TOK_DEV, KVW)

    def one_group(members):
        inputs_group, grads_group, error_group = members
        return jnp.dot(inputs_group.T.astype(jnp.float32), grads_group.astype(jnp.float32), preferred_element_type=jnp.float32) + error_group.astype(jnp.float32)
    summed = lax.map(one_group, (inputs_groups, grads_groups, error_section))
    block_width = KVW // N_TP
    results = []
    for which_block in range(N_TP):
        first_col = which_block * block_width
        columns = summed[:, :, first_col:first_col + block_width]
        coeffs_block = coeffs_prev[first_col:first_col + block_width]
        factor = jnp.einsum('gdk,kr->dr', columns, coeffs_block, precision=HIGHEST) / N_DP
        gram_matrix = jnp.dot(factor.T, factor, precision=HIGHEST)
        lower_factor = jnp.linalg.cholesky(gram_matrix)
        basis = jax.scipy.linalg.solve_triangular(lower_factor, factor.T, lower=True).T
        results.append(jnp.einsum('gdk,dr->kr', columns, basis, precision=HIGHEST) / N_DP)
    return jnp.concatenate(results, 0)

def reference(activations, key_grads, key_weight, error_buf, q_prev):
    input_grad = lax.map(section_gradient, (key_grads, key_weight))
    grad_prev = jnp.concatenate([input_grad[1:], jnp.zeros_like(input_grad[:1])], 0)
    q_new = lax.map(section_factors, (activations, key_grads, error_buf, q_prev))
    return (grad_prev, q_new)
```

```python
import jax
import jax.numpy as jnp
from jax import lax
from jax.experimental import pallas as pl
from jax.experimental.pallas import tpu as pltpu
from jax.sharding import Mesh
from jax.sharding import PartitionSpec as P

HIGHEST = lax.Precision.HIGHEST
BF16 = jnp.bfloat16
F32 = jnp.float32
GROUP = ("z", "c")


def swap(block, axis):
    return lax.ppermute(block, axis, [(0, 1), (1, 0)])


def dot(a, b, contract):
    return lax.dot_general(a, b, (contract, ((), ())), preferred_element_type=F32)


def split(values):
    high = values.astype(BF16)
    return jnp.concatenate([high, (values - high.astype(F32)).astype(BF16)], axis=1)


def finish_kernel(groups, gathered_ref, out_ref):
    rank = out_ref.shape[1]
    tall = out_ref.shape[0] // 2
    total = gathered_ref[0, :tall].astype(F32)
    for member in range(1, groups):
        total += gathered_ref[member, :tall].astype(F32)
    pair = gathered_ref[0, tall:].astype(F32) + gathered_ref[1, tall:].astype(F32)
    gram = pair[:, :rank] + pair[:, rank:]
    rows = lax.broadcasted_iota(jnp.int32, (rank, 2 * rank), 0)
    lanes = lax.broadcasted_iota(jnp.int32, (rank, 2 * rank), 1)
    identity = (lanes - rank == rows).astype(F32)
    work = jnp.concatenate([gram, gram], axis=1)
    work = jnp.where(lanes < rank, work, identity)
    for step in range(rank - 1):
        top = step // 8 * 8
        active = work[top:]
        column = jnp.broadcast_to(active[:, step : step + 1], active.shape)
        pivot_row = active[step - top : step - top + 1]
        pivot = column[step - top : step - top + 1]
        scaled = pivot_row / pivot
        active = active - jnp.where(rows[top:] > step, column, 0.0) * scaled
        work = active if top == 0 else jnp.concatenate([work[:top], active], axis=0)
    diagonal = jnp.sum(jnp.where(lanes == rows, work, 0.0), axis=1, keepdims=True)
    inverse = (work * lax.rsqrt(diagonal))[:, rank:]
    scale = 1.0 / groups
    for part in range(2):
        coeffs = total[:, part * rank : (part + 1) * rank] * scale
        out_ref[part * tall : (part + 1) * tall] = lax.dot_general(
            coeffs, inverse, (((1,), (1,)), ((), ())), precision=HIGHEST, preferred_element_type=F32
        )


def finish(gathered, kept, rank):
    return pl.pallas_call(
        lambda gathered_ref, out_ref: finish_kernel(gathered.shape[0], gathered_ref, out_ref),
        out_shape=jax.ShapeDtypeStruct((kept, rank), F32),
        name="finish",
    )(gathered)


def weight_route(chips, cores, sections):
    half = chips // 2

    def index(z, c, s, t):
        return ((z * cores + c) * sections + s) * 2 + t

    route = []
    for s in range(sections - 1):
        for z in range(chips):
            for c in range(cores):
                for t in range(2):
                    source = index(half * t + z % half, c, s + 1, t if z < half else 1 - t)
                    route.append((source, index(z, c, s, t)))
    return route


def on_device(activations, key_grads, key_weight, error_buf, q_prev):
    chips, cores, sections = (lax.axis_size(name) for name in ("z", "c", "pp"))
    groups = chips * cores
    core, side = lax.axis_index("c"), lax.axis_index("tp")
    inputs_local, grads_local, weight_local = activations[0], key_grads[0], key_weight[0]
    rank = q_prev.shape[2]
    tokens, features = inputs_local.shape
    part = features // cores
    columns = grads_local.shape[1]
    error_local = error_buf[0, 0].reshape(2, cores, part, columns)

    packed = jnp.concatenate([grads_local, split(q_prev[0])], axis=1)
    packed_near = swap(packed, "tp")
    inputs_mine = lax.dynamic_slice_in_dim(inputs_local, core * part, part, 1)
    inputs_other = lax.dynamic_slice_in_dim(inputs_local, (1 - core) * part, part, 1)
    inputs_pair = swap(inputs_other, "c")
    error_mine = lax.dynamic_index_in_dim(error_local, core, 1, keepdims=False)
    error_other = lax.dynamic_index_in_dim(error_local, 1 - core, 1, keepdims=False)
    error_pair = swap(error_other, "c")
    q_own, q_near = packed[:, columns:], packed_near[:, columns:]
    grads_near = packed_near[:, :columns]
    grads_both = jnp.stack([grads_local, grads_near])
    grads_pair = swap(grads_both, "c")

    weight_piece = lax.ppermute(
        weight_local, ("z", "c", "pp", "tp"), weight_route(chips, cores, sections)
    )
    weight_all = lax.all_gather(weight_piece, GROUP, axis=0, tiled=False)
    grads_next = lax.ppermute(grads_both, "pp", [(i, i - 1) for i in range(1, sections)])
    weight_own = weight_all[: groups // 2].reshape(features, columns)
    weight_near = weight_all[groups // 2 :].reshape(features, columns)
    grad_prev = (
        dot(grads_next[0], weight_own, ((1,), (1,))) + dot(grads_next[1], weight_near, ((1,), (1,)))
    ).astype(BF16)

    tall = ((0,), (0,))
    product_near = (
        dot(inputs_mine, grads_near, tall) + dot(inputs_pair, grads_pair[1], tall)
    ).astype(BF16)
    product_own = (
        dot(inputs_mine, grads_local, tall) + dot(inputs_pair, grads_pair[0], tall)
    ).astype(BF16)
    wide = ((1,), (0,))

    def times_q(block, q):
        both = dot(block, q, wide)
        return both[:, :rank] + both[:, rank:]

    factor_from_near = swap(times_q(product_near, q_near).astype(BF16), "tp").astype(F32)
    product_from_near = swap(product_near, "tp")
    factor_own = times_q(product_own, q_own)
    factor_error = [
        times_q(error_mine[half], q_own) + times_q(error_pair[half], q_own) for half in range(2)
    ]
    first = side == 0
    factor = jnp.concatenate(
        [
            factor_error[0] + jnp.where(first, factor_own, factor_from_near),
            factor_error[1] + jnp.where(first, factor_from_near, factor_own),
        ],
        axis=1,
    )
    shares = (factor / groups).astype(BF16).reshape(chips, part // chips, 2 * rank)
    shares = lax.all_to_all(shares, "z", 0, 0)
    share = jnp.sum(shares.astype(F32), axis=0).astype(BF16)
    factor = lax.all_to_all(jnp.broadcast_to(share, (chips, *share.shape)), "z", 0, 0)
    factor = factor.reshape(part, 2 * rank)

    gram_pair = dot(factor, factor, tall)
    gram = gram_pair[:rank, :rank] + gram_pair[rank:, rank:]
    product = [
        jnp.where(first, product_own, product_from_near),
        jnp.where(first, product_from_near, product_own),
    ]
    coeffs = 0.0
    for half in range(2):
        summed = (
            error_mine[half].astype(F32) + error_pair[half].astype(F32) + product[half].astype(F32)
        ).astype(BF16)
        coeffs += dot(summed, factor[:, half * rank : (half + 1) * rank], tall)
    kept = columns // 2
    coeffs = jnp.concatenate([coeffs[:kept], coeffs[kept:]], axis=1).astype(BF16)
    payload = jnp.concatenate([coeffs, split(gram)], axis=0)
    gathered = lax.all_gather(payload, GROUP, axis=0, tiled=False)
    return (grad_prev[None], finish(gathered, columns, rank)[None])


def solution(mesh):
    groups, sections, sides = (mesh.shape[name] for name in ("dp", "pp", "tp"))
    split_mesh = Mesh(
        mesh.devices.reshape(groups // 2, 2, sections, sides), ("z", "c", "pp", "tp")
    )
    return jax.shard_map(
        on_device,
        mesh=split_mesh,
        in_specs=(
            P("pp", GROUP, "tp"),
            P("pp", GROUP, "tp"),
            P("pp", GROUP, "tp"),
            P("pp", GROUP, None, "tp"),
            P("pp", "tp", None),
        ),
        out_specs=(P("pp", GROUP, "tp"), P("pp", "tp", None)),
        check_vma=False,
    )
```

```python
import jax
import jax.numpy as jnp
from jax import lax
from jax.experimental import pallas as pl
from jax.experimental.pallas import tpu as pltpu
from jax.sharding import Mesh
from jax.sharding import PartitionSpec as P

HIGHEST = lax.Precision.HIGHEST
BF16 = jnp.bfloat16
F32 = jnp.float32
GROUP = ("z", "c")
VMEM_LIMIT = 12 * 2**20
VMEM_ALL = 60 * 2**20
STEP = 512
WIDE = 4


def swap(block, axis):
    return lax.ppermute(block, axis, [(0, 1), (1, 0)])


def dot(a, b, a_dim=1, b_dim=0):
    return lax.dot_general(a, b, (((a_dim,), (b_dim,)), ((), ())), preferred_element_type=F32)


def split(values, axis):
    high = values.astype(BF16)
    return jnp.concatenate([high, (values - high.astype(F32)).astype(BF16)], axis=axis)


def place(name):
    return lax.axis_index(name).astype(jnp.int32).reshape(1)


def call(kernel, out_shapes, name, operands, scalars=1, flops=10**8, moved=4 * 10**6):
    spaces = [pltpu.SMEM] * scalars + [pltpu.VMEM] * (len(operands) - scalars)
    return pl.pallas_call(
        kernel,
        out_shape=out_shapes,
        in_specs=[pl.BlockSpec(memory_space=space) for space in spaces],
        cost_estimate=pl.CostEstimate(flops=flops, bytes_accessed=moved, transcendentals=0),
        compiler_params=pltpu.CompilerParams(vmem_limit_bytes=VMEM_LIMIT),
        name=name,
    )(*operands)


def times_q(q_parts, block):
    rank = q_parts.shape[0] // 2
    both = dot(q_parts, block, 1, 1)
    return both[:rank] + both[rank:]


def project_kernel(
    side_ref, q_hbm, grads_hbm, error_hbm, payload_ref, q_ref, grads_ref, error_ref, arrived
):
    features, tokens = error_ref.shape[0], grads_ref.shape[0]
    away = pl.ds(pl.multiple_of((1 - side_ref[0]) * features, features), features)
    sources = (q_hbm, grads_hbm, error_hbm.at[away])
    targets = (q_ref, grads_ref, error_ref)
    copies = [pltpu.make_async_copy(*sources_targets, arrived.at[i])
              for i, sources_targets in enumerate(zip(sources, targets))]
    for copy in copies:
        copy.start()
    copies[0].wait()
    q_parts = split(q_ref[...], 0)
    copies[1].wait()
    payload_ref[:, features:] = times_q(q_parts, grads_ref[...]).astype(BF16)
    copies[2].wait()
    for start in range(0, features, STEP):
        rows = slice(start, start + STEP)
        payload_ref[:, rows] = times_q(q_parts, error_ref[rows]).astype(BF16)


def project(side, q_prev, grads, error):
    rank, columns = q_prev.shape
    tokens, features = grads.shape[0], error.shape[0] // 2
    hbm = pl.BlockSpec(memory_space=pltpu.HBM)
    return pl.pallas_call(
        project_kernel,
        out_shape=jax.ShapeDtypeStruct((rank, features + tokens), BF16),
        in_specs=[pl.BlockSpec(memory_space=pltpu.SMEM), hbm, hbm, hbm],
        out_specs=pl.BlockSpec(memory_space=pltpu.VMEM),
        scratch_shapes=[
            pltpu.VMEM((rank, columns), F32),
            pltpu.VMEM((tokens, columns), BF16),
            pltpu.VMEM((features, columns), BF16),
            pltpu.SemaphoreType.DMA((3,)),
        ],
        cost_estimate=pl.CostEstimate(flops=10**8, bytes_accessed=2 * 10**6, transcendentals=0),
        compiler_params=pltpu.CompilerParams(vmem_limit_bytes=VMEM_ALL),
        name="project",
    )(side, q_prev, grads, error)


def left_kernel(groups, side_ref, pair_ref, q_ref, error_ref, inputs_ref, out_ref):
    features, side = inputs_ref.shape[1], side_ref[0]
    rank = q_ref.shape[0]
    payload_ref, near_ref = pair_ref.at[side], pair_ref.at[1 - side]
    q_parts = split(q_ref[...], 0)
    mixed = jnp.concatenate([payload_ref[:, features:], near_ref[:, features:]], axis=0)
    for start in range(0, features, STEP):
        lanes = slice(start, start + STEP)
        rows = pl.ds(pl.multiple_of(side * features + start, STEP), STEP)
        product = dot(mixed, inputs_ref[:, lanes])
        own = (product[:rank] + times_q(q_parts, error_ref[rows])) * (1.0 / groups)
        near = (product[rank:] + near_ref[:, lanes].astype(F32)) * (1.0 / groups)
        out_ref[0, :, lanes] = own.astype(BF16)
        out_ref[1, :, lanes] = near.astype(BF16)


def chip_sum_kernel(pair_ref, out_ref):
    chunks, _, width = out_ref.shape
    for chunk in range(chunks):
        lanes = slice(chunk * width, (chunk + 1) * width)
        total = pair_ref[0, :, lanes].astype(F32) + pair_ref[1, :, lanes].astype(F32)
        out_ref[chunk] = total.astype(BF16)


def share_kernel(shares_ref, out_ref):
    groups = shares_ref.shape[0]
    for core in range(2):
        total = shares_ref[core].astype(F32)
        for member in range(core + 2, groups, 2):
            total += shares_ref[member].astype(F32)
        total = total.astype(BF16)
        for member in range(core, groups, 2):
            out_ref[member] = total


def right_kernel(
    side_ref, factor_ref, inputs_ref, near_ref, error_ref, away_ref, projected_ref, own_ref, gram_ref
):
    _, chunks, rank, width = factor_ref.shape
    side = side_ref[0]
    tokens, features = inputs_ref.shape
    columns = own_ref.shape[1]
    projected = jnp.zeros((2 * rank, tokens), F32)
    gram = jnp.zeros((2 * rank, 2 * rank), F32)
    own = jnp.zeros((rank, columns), F32)
    near = jnp.zeros((rank, columns), F32)
    for chunk in range(0, chunks, 2):
        factor = jnp.concatenate(
            [
                jnp.concatenate([factor_ref[block, chunk + i] for i in range(2)], axis=1)
                for block in range(2)
            ],
            axis=0,
        )
        lanes = slice(chunk * width, (chunk + 2) * width)
        projected += dot(factor, inputs_ref[:, lanes], 1, 1)
        gram += dot(factor, factor, 1, 1)
        near += dot(factor[rank:], near_ref[lanes])
        start, size = chunk * width, 2 * width
        rows = pl.ds(pl.multiple_of(side * features + start, size), size)
        own += dot(factor[:rank], error_ref[rows])
    away_ref[:, :tokens] = projected[rank:].astype(BF16)
    away_ref[:, tokens : tokens + columns] = near.astype(BF16)
    away_ref[:, tokens + columns :] = split(gram[rank:, rank:], 1)
    projected_ref[...] = projected[:rank]
    own_ref[...] = own
    gram_ref[...] = gram[:rank, :rank]


def join_kernel(side_ref, pair_ref, projected_ref, own_ref, grads_ref, out_ref):
    tokens, columns = grads_ref.shape
    near = pair_ref[1 - side_ref[0]].astype(F32)
    projected = (projected_ref[...] + near[:, :tokens]).astype(BF16)
    total = own_ref[...] + near[:, tokens : tokens + columns]
    out_ref[...] = (total + dot(projected, grads_ref[...])).astype(BF16)


def spread_kernel(core_ref, pair_ref, out_ref):
    copies, _, width = out_ref.shape
    lanes = pl.ds(pl.multiple_of(core_ref[0] * width, width), width)
    total = pair_ref[0, :, lanes].astype(F32) + pair_ref[1, :, lanes].astype(F32)
    total = total.astype(BF16)
    for copy in range(copies):
        out_ref[copy] = total


def invert_kernel(side_ref, pair_ref, own_ref, out_ref):
    rank = out_ref.shape[0]
    start = pair_ref.shape[2] - 2 * rank
    near = pair_ref[1 - side_ref[0], :, start:].astype(F32)
    gram = own_ref[...] + near[:, :rank] + near[:, rank:]
    rows = lax.broadcasted_iota(jnp.int32, (rank, 2 * rank), 0)
    lanes = lax.broadcasted_iota(jnp.int32, (rank, 2 * rank), 1)
    identity = (lanes - rank == rows).astype(F32)
    work = jnp.concatenate([gram, gram], axis=1)
    work = jnp.where(lanes < rank, work, identity)
    for start in range(0, rank, WIDE):
        top = start // 8 * 8
        active = work[top:]
        columns = [
            jnp.broadcast_to(active[:, start + i : start + i + 1], active.shape)
            for i in range(WIDE)
        ]
        for i in range(WIDE):
            row = start + i - top
            scale = 1.0 / columns[i][row : row + 1]
            below = jnp.where(rows[top:] > start + i, columns[i], 0.0)
            for j in range(i + 1, WIDE):
                across = columns[i][row + j - i : row + j - i + 1] * scale
                columns[j] = columns[j] - below * across
            active = active - below * (active[row : row + 1] * scale)
        work = active if top == 0 else jnp.concatenate([work[:top], active], axis=0)
    diagonal = jnp.sum(jnp.where(lanes == rows, work, 0.0), axis=1, keepdims=True)
    out_ref[...] = (work * lax.rsqrt(diagonal))[:, rank:]


def finish_kernel(gathered_ref, inverse_ref, out_ref):
    members, _, width = gathered_ref.shape
    cores = out_ref.shape[1] // width
    for core in range(cores):
        total = gathered_ref[core].astype(F32)
        for member in range(core + cores, members, cores):
            total += gathered_ref[member].astype(F32)
        out_ref[:, core * width : (core + 1) * width] = jnp.dot(
            inverse_ref[...], total * (1.0 / members), precision=HIGHEST, preferred_element_type=F32
        )


def input_grad_kernel(side_ref, grads_ref, grads_near_ref, weight_ref, out_ref):
    step, side = pl.program_id(0), side_ref[0]
    half = weight_ref.shape[0] // 2
    own = weight_ref[(1 - side) * half + half - 1 - step]
    near = weight_ref[side * half + step]
    total = dot(grads_ref[...], own, 1, 1) + dot(grads_near_ref[...], near, 1, 1)
    out_ref[...] = total.astype(BF16)


def input_grad(side, grads, grads_near, weight):
    tokens, _ = grads.shape
    pieces, rows, _ = weight.shape
    vmem = pl.BlockSpec(memory_space=pltpu.VMEM)
    return pl.pallas_call(
        input_grad_kernel,
        out_shape=jax.ShapeDtypeStruct((tokens, pieces // 2 * rows), BF16),
        grid=(pieces // 2,),
        in_specs=[pl.BlockSpec(memory_space=pltpu.SMEM), vmem, vmem, vmem],
        out_specs=pl.BlockSpec((tokens, rows), lambda step: (0, step)),
        cost_estimate=pl.CostEstimate(flops=10**9, bytes_accessed=3 * 10**6, transcendentals=0),
        compiler_params=pltpu.CompilerParams(vmem_limit_bytes=VMEM_LIMIT),
        name="input_grad",
    )(side, grads, grads_near, weight)


def weight_route(chips, cores, sections):
    def index(z, c, s, t):
        return ((z * cores + c) * sections + s) * 2 + t

    route = []
    for s in range(sections - 1):
        for z in range(chips):
            for c in range(cores):
                for t in range(2):
                    if z // (chips // 2) == t:
                        source = index(z, c, s + 1, 1 - t)
                    else:
                        source = index(chips - 1 - z, c, s + 1, t)
                    route.append((source, index(z, c, s, t)))
    return route


def on_device(activations, key_grads, key_weight, error_buf, q_prev):
    chips, cores, sections = (lax.axis_size(name) for name in ("z", "c", "pp"))
    groups = chips * cores
    side, core = place("tp"), place("c")
    inputs, grads, weight, error = activations[0], key_grads[0], key_weight[0], error_buf[0, 0]
    rank = q_prev.shape[2]
    tokens, features = inputs.shape
    columns = grads.shape[1]
    part = features // groups

    def shape(*sizes, kind=F32):
        return jax.ShapeDtypeStruct(sizes, kind)

    weight_piece = lax.ppermute(
        weight, ("z", "c", "pp", "tp"), weight_route(chips, cores, sections)
    )

    q_rows = q_prev[0].T
    payload = project(side, q_rows, grads, error)
    payload = lax.all_gather(payload, "tp", axis=0, tiled=False)
    payload, weight_piece = lax.optimization_barrier((payload, weight_piece))
    weight_all = lax.all_gather(weight_piece, GROUP, axis=0, tiled=False)
    factor = call(
        lambda *refs: left_kernel(groups, *refs),
        shape(cores, rank, features, kind=BF16),
        "left",
        (side, payload, q_rows, error, inputs),
    )
    factor = lax.all_to_all(factor, "c", 0, 0)
    shares = call(
        chip_sum_kernel,
        shape(groups, rank, part, kind=BF16),
        "chip_sum",
        (factor,),
        scalars=0,
    )
    shares, error_later = lax.optimization_barrier((shares, error))
    shares = lax.all_to_all(shares, GROUP, 0, 0)
    error_near = swap(
        lax.dynamic_slice_in_dim(error_later, (1 - side[0]) * features, features, 0), "tp"
    )
    spread = call(
        share_kernel, shape(groups, rank, part, kind=BF16), "share", (shares,), scalars=0
    )
    spread, grads_later = lax.optimization_barrier((spread, grads))
    factor = lax.all_to_all(spread, GROUP, 0, 0)
    grads_next = lax.ppermute(grads_later, "pp", [(i, i - 1) for i in range(1, sections)])
    grads_next_near = lax.ppermute(
        grads_later,
        ("pp", "tp"),
        [(2 * s + 2 + 1 - t, 2 * s + t) for s in range(sections - 1) for t in range(2)],
    )
    factor = lax.all_gather(factor, "c", axis=0, tiled=False)

    away, projected, coeffs, gram = call(
        right_kernel,
        (
            shape(rank, tokens + columns + 2 * rank, kind=BF16),
            shape(rank, tokens),
            shape(rank, columns),
            shape(rank, rank),
        ),
        "right",
        (side, factor, inputs, error_near, error),
    )
    pair = lax.all_gather(away, "tp", axis=0, tiled=False)
    pair, grads_next, grads_next_near = lax.optimization_barrier(
        (pair, grads_next, grads_next_near)
    )
    coeffs = call(
        join_kernel,
        shape(rank, columns, kind=BF16),
        "join",
        (side, pair, projected, coeffs, grads),
    )
    coeffs = lax.all_gather(coeffs, "c", axis=0, tiled=False)
    spread = call(
        spread_kernel, shape(groups, rank, columns // cores, kind=BF16), "spread", (core, coeffs)
    )
    gathered = lax.all_to_all(spread, GROUP, 0, 0)
    inverse = call(invert_kernel, shape(rank, rank), "invert", (side, pair, gram))
    grad_prev = input_grad(
        side, grads_next, grads_next_near, weight_all.reshape(chips, cores * tokens, columns)
    )
    gathered, inverse, grad_prev = lax.optimization_barrier((gathered, inverse, grad_prev))
    coeffs = call(finish_kernel, shape(rank, columns), "finish", (gathered, inverse), scalars=0)
    return (grad_prev[None], coeffs.T[None])


def solution(mesh):
    groups, sections, sides = (mesh.shape[name] for name in ("dp", "pp", "tp"))
    split_mesh = Mesh(
        mesh.devices.reshape(groups // 2, 2, sections, sides), ("z", "c", "pp", "tp")
    )
    return jax.shard_map(
        on_device,
        mesh=split_mesh,
        in_specs=(
            P("pp", GROUP, "tp"),
            P("pp", GROUP, "tp"),
            P("pp", GROUP, "tp"),
            P("pp", GROUP, None, "tp"),
            P("pp", "tp", None),
        ),
        out_specs=(P("pp", GROUP, "tp"), P("pp", "tp", None)),
        check_vma=False,
    )
```

```python
import jax
import jax.numpy as jnp
from jax import lax
from jax.experimental import pallas as pl
from jax.experimental.pallas import tpu as pltpu
from jax.sharding import Mesh
from jax.sharding import PartitionSpec as P

HIGHEST = lax.Precision.HIGHEST
BF16 = jnp.bfloat16
F32 = jnp.float32
GROUP = ("z", "c")
VMEM_LIMIT = 12 * 2**20
VMEM_ALL = 60 * 2**20
STEP = 512
WIDE = 4


def swap(block, axis):
    return lax.ppermute(block, axis, [(0, 1), (1, 0)])


def dot(a, b, a_dim=1, b_dim=0):
    return lax.dot_general(a, b, (((a_dim,), (b_dim,)), ((), ())), preferred_element_type=F32)


def split(values, axis):
    high = values.astype(BF16)
    return jnp.concatenate([high, (values - high.astype(F32)).astype(BF16)], axis=axis)


def place(name):
    return lax.axis_index(name).astype(jnp.int32).reshape(1)


def call(kernel, out_shapes, name, operands, scalars=1, flops=10**8, moved=4 * 10**6):
    spaces = [pltpu.SMEM] * scalars + [pltpu.VMEM] * (len(operands) - scalars)
    return pl.pallas_call(
        kernel,
        out_shape=out_shapes,
        in_specs=[pl.BlockSpec(memory_space=space) for space in spaces],
        cost_estimate=pl.CostEstimate(flops=flops, bytes_accessed=moved, transcendentals=0),
        compiler_params=pltpu.CompilerParams(vmem_limit_bytes=VMEM_LIMIT),
        name=name,
    )(*operands)


def times_q(q_parts, block):
    rank = q_parts.shape[0] // 2
    both = dot(q_parts, block, 1, 1)
    return both[:rank] + both[rank:]


def project_kernel(
    side_ref, q_hbm, grads_hbm, error_hbm, payload_ref, q_ref, grads_ref, error_ref, arrived
):
    features, tokens = error_ref.shape[0], grads_ref.shape[0]
    away = pl.ds(pl.multiple_of((1 - side_ref[0]) * features, features), features)
    sources = (q_hbm, grads_hbm, error_hbm.at[away])
    targets = (q_ref, grads_ref, error_ref)
    copies = [pltpu.make_async_copy(*sources_targets, arrived.at[i])
              for i, sources_targets in enumerate(zip(sources, targets))]
    for copy in copies:
        copy.start()
    copies[0].wait()
    q_parts = split(q_ref[...], 0)
    copies[1].wait()
    payload_ref[:, features:] = times_q(q_parts, grads_ref[...]).astype(BF16)
    copies[2].wait()
    for start in range(0, features, STEP):
        rows = slice(start, start + STEP)
        payload_ref[:, rows] = times_q(q_parts, error_ref[rows]).astype(BF16)


def project(side, q_prev, grads, error):
    rank, columns = q_prev.shape
    tokens, features = grads.shape[0], error.shape[0] // 2
    hbm = pl.BlockSpec(memory_space=pltpu.HBM)
    return pl.pallas_call(
        project_kernel,
        out_shape=jax.ShapeDtypeStruct((rank, features + tokens), BF16),
        in_specs=[pl.BlockSpec(memory_space=pltpu.SMEM), hbm, hbm, hbm],
        out_specs=pl.BlockSpec(memory_space=pltpu.VMEM),
        scratch_shapes=[
            pltpu.VMEM((rank, columns), F32),
            pltpu.VMEM((tokens, columns), BF16),
            pltpu.VMEM((features, columns), BF16),
            pltpu.SemaphoreType.DMA((3,)),
        ],
        cost_estimate=pl.CostEstimate(flops=10**8, bytes_accessed=2 * 10**6, transcendentals=0),
        compiler_params=pltpu.CompilerParams(vmem_limit_bytes=VMEM_ALL),
        name="project",
    )(side, q_prev, grads, error)


def left_kernel(groups, side_ref, pair_ref, q_ref, error_ref, inputs_ref, out_ref):
    features, side = inputs_ref.shape[1], side_ref[0]
    rank = q_ref.shape[0]
    payload_ref, near_ref = pair_ref.at[side], pair_ref.at[1 - side]
    q_parts = split(q_ref[...], 0)
    mixed = jnp.concatenate([payload_ref[:, features:], near_ref[:, features:]], axis=0)
    for start in range(0, features, STEP):
        lanes = slice(start, start + STEP)
        rows = pl.ds(pl.multiple_of(side * features + start, STEP), STEP)
        product = dot(mixed, inputs_ref[:, lanes])
        own = (product[:rank] + times_q(q_parts, error_ref[rows])) * (1.0 / groups)
        near = (product[rank:] + near_ref[:, lanes].astype(F32)) * (1.0 / groups)
        out_ref[0, :, lanes] = own.astype(BF16)
        out_ref[1, :, lanes] = near.astype(BF16)


def chip_sum_kernel(pair_ref, out_ref):
    chunks, _, width = out_ref.shape
    for chunk in range(chunks):
        lanes = slice(chunk * width, (chunk + 1) * width)
        total = pair_ref[0, :, lanes].astype(F32) + pair_ref[1, :, lanes].astype(F32)
        out_ref[chunk] = total.astype(BF16)


def share_kernel(shares_ref, out_ref):
    groups, rank, _ = shares_ref.shape
    for core in range(2):
        total = shares_ref[core].astype(F32)
        for member in range(core + 2, groups, 2):
            total += shares_ref[member].astype(F32)
        out_ref[core * rank : (core + 1) * rank] = total.astype(BF16)


def two_chunks(factor_ref, chunk, rows):
    return jnp.concatenate([factor_ref[chunk, rows], factor_ref[chunk + 1, rows]], axis=1)


def right_kernel(core_ref, factor_ref, inputs_ref, away_ref, projected_ref, gram_ref):
    chunks, both, width = factor_ref.shape
    rank, half = both // 2, chunks // 2
    tokens = inputs_ref.shape[0]
    projected = jnp.zeros((both, tokens), F32)
    gram = jnp.zeros((both, both), F32)
    for chunk in range(0, chunks, 2):
        factor = two_chunks(factor_ref, chunk, slice(None))
        projected += dot(factor, inputs_ref[:, chunk * width : (chunk + 2) * width], 1, 1)
        gram += dot(factor, factor, 1, 1)
    for chunk in range(half):
        lanes = slice(chunk * width, (chunk + 1) * width)
        away_ref[:, lanes] = factor_ref[core_ref[0] * half + chunk, rank:]
    start = half * width
    away_ref[:, start : start + tokens] = projected[rank:].astype(BF16)
    away_ref[:, start + tokens :] = split(gram[rank:, rank:], 1)
    projected_ref[...] = projected[:rank]
    gram_ref[...] = gram[:rank, :rank]


def join_kernel(
    side_ref, core_ref, pair_ref, factor_ref, projected_ref, grads_ref, error_ref, error_pair_ref,
    out_ref,
):
    chunks, both, width = factor_ref.shape
    rank, tokens = both // 2, grads_ref.shape[0]
    features, part = chunks * width, error_pair_ref.shape[0]
    side = side_ref[0]
    near_ref = pair_ref.at[1 - side]
    near = near_ref[:, part : part + tokens].astype(F32)
    total = dot((projected_ref[...] + near).astype(BF16), grads_ref[...])
    size = 2 * width
    for start in range(0, features, size):
        rows = pl.ds(pl.multiple_of(side * features + start, size), size)
        total += dot(two_chunks(factor_ref, start // width, slice(rank)), error_ref[rows])
    for start in range(0, part, size):
        lanes = slice(start, start + size)
        first = (1 - side) * features + core_ref[0] * part + start
        rows = pl.ds(pl.multiple_of(first, size), size)
        total += dot(near_ref[:, lanes], error_ref[rows])
        total += dot(near_ref[:, lanes], error_pair_ref[lanes])
    out_ref[...] = total.astype(BF16)


def spread_kernel(core_ref, pair_ref, out_ref):
    copies, _, width = out_ref.shape
    lanes = pl.ds(pl.multiple_of(core_ref[0] * width, width), width)
    total = pair_ref[0, :, lanes].astype(F32) + pair_ref[1, :, lanes].astype(F32)
    total = total.astype(BF16)
    for copy in range(copies):
        out_ref[copy] = total


def invert_kernel(side_ref, pair_ref, own_ref, out_ref):
    rank = out_ref.shape[0]
    start = pair_ref.shape[2] - 2 * rank
    near = pair_ref[1 - side_ref[0], :, start:].astype(F32)
    gram = own_ref[...] + near[:, :rank] + near[:, rank:]
    rows = lax.broadcasted_iota(jnp.int32, (rank, 2 * rank), 0)
    lanes = lax.broadcasted_iota(jnp.int32, (rank, 2 * rank), 1)
    identity = (lanes - rank == rows).astype(F32)
    work = jnp.concatenate([gram, gram], axis=1)
    work = jnp.where(lanes < rank, work, identity)
    for start in range(0, rank, WIDE):
        top = start // 8 * 8
        active = work[top:]
        columns = [
            jnp.broadcast_to(active[:, start + i : start + i + 1], active.shape)
            for i in range(WIDE)
        ]
        for i in range(WIDE):
            row = start + i - top
            scale = 1.0 / columns[i][row : row + 1]
            below = jnp.where(rows[top:] > start + i, columns[i], 0.0)
            for j in range(i + 1, WIDE):
                across = columns[i][row + j - i : row + j - i + 1] * scale
                columns[j] = columns[j] - below * across
            active = active - below * (active[row : row + 1] * scale)
        work = active if top == 0 else jnp.concatenate([work[:top], active], axis=0)
    diagonal = jnp.sum(jnp.where(lanes == rows, work, 0.0), axis=1, keepdims=True)
    out_ref[...] = (work * lax.rsqrt(diagonal))[:, rank:]


def finish_kernel(gathered_ref, inverse_ref, out_ref):
    members, _, width = gathered_ref.shape
    cores = out_ref.shape[1] // width
    for core in range(cores):
        total = gathered_ref[core].astype(F32)
        for member in range(core + cores, members, cores):
            total += gathered_ref[member].astype(F32)
        out_ref[:, core * width : (core + 1) * width] = jnp.dot(
            inverse_ref[...], total * (1.0 / members), precision=HIGHEST, preferred_element_type=F32
        )


def input_grad_kernel(side_ref, grads_ref, grads_near_ref, weight_ref, out_ref):
    step, side = pl.program_id(0), side_ref[0]
    half = weight_ref.shape[0] // 2
    own = weight_ref[(1 - side) * half + half - 1 - step]
    near = weight_ref[side * half + step]
    total = dot(grads_ref[...], own, 1, 1) + dot(grads_near_ref[...], near, 1, 1)
    out_ref[...] = total.astype(BF16)


def input_grad(side, grads, grads_near, weight):
    tokens, _ = grads.shape
    pieces, rows, _ = weight.shape
    vmem = pl.BlockSpec(memory_space=pltpu.VMEM)
    return pl.pallas_call(
        input_grad_kernel,
        out_shape=jax.ShapeDtypeStruct((tokens, pieces // 2 * rows), BF16),
        grid=(pieces // 2,),
        in_specs=[pl.BlockSpec(memory_space=pltpu.SMEM), vmem, vmem, vmem],
        out_specs=pl.BlockSpec((tokens, rows), lambda step: (0, step)),
        cost_estimate=pl.CostEstimate(flops=10**9, bytes_accessed=3 * 10**6, transcendentals=0),
        compiler_params=pltpu.CompilerParams(vmem_limit_bytes=VMEM_LIMIT),
        name="input_grad",
    )(side, grads, grads_near, weight)


def weight_route(chips, cores, sections):
    def index(z, c, s, t):
        return ((z * cores + c) * sections + s) * 2 + t

    route = []
    for s in range(sections - 1):
        for z in range(chips):
            for c in range(cores):
                for t in range(2):
                    if z // (chips // 2) == t:
                        source = index(z, c, s + 1, 1 - t)
                    else:
                        source = index(chips - 1 - z, c, s + 1, t)
                    route.append((source, index(z, c, s, t)))
    return route


def on_device(activations, key_grads, key_weight, error_buf, q_prev):
    chips, cores, sections = (lax.axis_size(name) for name in ("z", "c", "pp"))
    groups = chips * cores
    side, core = place("tp"), place("c")
    inputs, grads, weight, error = activations[0], key_grads[0], key_weight[0], error_buf[0, 0]
    rank = q_prev.shape[2]
    tokens, features = inputs.shape
    columns = grads.shape[1]
    part = features // groups

    def shape(*sizes, kind=F32):
        return jax.ShapeDtypeStruct(sizes, kind)

    weight_piece = lax.ppermute(
        weight, ("z", "c", "pp", "tp"), weight_route(chips, cores, sections)
    )

    q_rows = q_prev[0].T
    payload = project(side, q_rows, grads, error)
    payload = lax.all_gather(payload, "tp", axis=0, tiled=False)
    payload, weight_piece = lax.optimization_barrier((payload, weight_piece))
    weight_all = lax.all_gather(weight_piece, GROUP, axis=0, tiled=False)
    factor = call(
        lambda *refs: left_kernel(groups, *refs),
        shape(cores, rank, features, kind=BF16),
        "left",
        (side, payload, q_rows, error, inputs),
    )
    factor = lax.all_to_all(factor, "c", 0, 0)
    shares = call(
        chip_sum_kernel,
        shape(groups, rank, part, kind=BF16),
        "chip_sum",
        (factor,),
        scalars=0,
    )
    shares, error_later, grads_later = lax.optimization_barrier((shares, error, grads))
    shares = lax.all_to_all(shares, GROUP, 0, 0)
    grads_next = lax.ppermute(grads_later, "pp", [(i, i - 1) for i in range(1, sections)])
    grads_next_near = lax.ppermute(
        grads_later,
        ("pp", "tp"),
        [(2 * s + 2 + 1 - t, 2 * s + t) for s in range(sections - 1) for t in range(2)],
    )
    error_part = features // cores
    error_away = (1 - side[0]) * features + (1 - core[0]) * error_part
    error_pair = swap(lax.dynamic_slice_in_dim(error_later, error_away, error_part, 0), "c")
    share = call(share_kernel, shape(2 * rank, part, kind=BF16), "share", (shares,), scalars=0)
    factor = lax.all_gather(share, GROUP, axis=0, tiled=False)
    factor, grads_next, grads_next_near, error_pair = lax.optimization_barrier(
        (factor, grads_next, grads_next_near, error_pair)
    )

    away, projected, gram = call(
        right_kernel,
        (
            shape(rank, error_part + tokens + 2 * rank, kind=BF16),
            shape(rank, tokens),
            shape(rank, rank),
        ),
        "right",
        (core, factor, inputs),
    )
    pair = lax.all_gather(away, "tp", axis=0, tiled=False)
    coeffs = call(
        join_kernel,
        shape(rank, columns, kind=BF16),
        "join",
        (side, core, pair, factor, projected, grads, error, error_pair),
        scalars=2,
    )
    coeffs = lax.all_gather(coeffs, "c", axis=0, tiled=False)
    spread = call(
        spread_kernel, shape(groups, rank, columns // cores, kind=BF16), "spread", (core, coeffs)
    )
    gathered = lax.all_to_all(spread, GROUP, 0, 0)
    inverse = call(invert_kernel, shape(rank, rank), "invert", (side, pair, gram))
    grad_prev = input_grad(
        side, grads_next, grads_next_near, weight_all.reshape(chips, cores * tokens, columns)
    )
    gathered, inverse, grad_prev = lax.optimization_barrier((gathered, inverse, grad_prev))
    coeffs = call(finish_kernel, shape(rank, columns), "finish", (gathered, inverse), scalars=0)
    return (grad_prev[None], coeffs.T[None])


def solution(mesh):
    groups, sections, sides = (mesh.shape[name] for name in ("dp", "pp", "tp"))
    split_mesh = Mesh(
        mesh.devices.reshape(groups // 2, 2, sections, sides), ("z", "c", "pp", "tp")
    )
    return jax.shard_map(
        on_device,
        mesh=split_mesh,
        in_specs=(
            P("pp", GROUP, "tp"),
            P("pp", GROUP, "tp"),
            P("pp", GROUP, "tp"),
            P("pp", GROUP, None, "tp"),
            P("pp", "tp", None),
        ),
        out_specs=(P("pp", GROUP, "tp"), P("pp", "tp", None)),
        check_vma=False,
    )
```

```python
import jax
import jax.numpy as jnp
from jax import lax
from jax.experimental import pallas as pl
from jax.experimental.pallas import tpu as pltpu
from jax.sharding import Mesh
from jax.sharding import PartitionSpec as P

HIGHEST = lax.Precision.HIGHEST
BF16 = jnp.bfloat16
F32 = jnp.float32
GROUP = ("z", "c")
VMEM_LIMIT = 12 * 2**20
VMEM_ALL = 60 * 2**20
STEP = 512
WIDE = 4


def swap(block, axis):
    return lax.ppermute(block, axis, [(0, 1), (1, 0)])


def dot(a, b, a_dim=1, b_dim=0):
    return lax.dot_general(a, b, (((a_dim,), (b_dim,)), ((), ())), preferred_element_type=F32)


def split(values, axis):
    high = values.astype(BF16)
    return jnp.concatenate([high, (values - high.astype(F32)).astype(BF16)], axis=axis)


def place(name):
    return lax.axis_index(name).astype(jnp.int32).reshape(1)


def call(kernel, out_shapes, name, operands, scalars=1, flops=10**8, moved=4 * 10**6):
    spaces = [pltpu.SMEM] * scalars + [pltpu.VMEM] * (len(operands) - scalars)
    return pl.pallas_call(
        kernel,
        out_shape=out_shapes,
        in_specs=[pl.BlockSpec(memory_space=space) for space in spaces],
        cost_estimate=pl.CostEstimate(flops=flops, bytes_accessed=moved, transcendentals=0),
        compiler_params=pltpu.CompilerParams(vmem_limit_bytes=VMEM_LIMIT),
        name=name,
    )(*operands)


def times_q(q_parts, block):
    rank = q_parts.shape[0] // 2
    both = dot(q_parts, block, 1, 1)
    return both[:rank] + both[rank:]


def project_kernel(
    side_ref, core_ref, q_hbm, grads_hbm, error_hbm, pair_hbm, payload_ref,
    q_ref, grads_ref, error_ref, arrived,
):
    part = pair_hbm.shape[0]
    features = error_hbm.shape[0] // 2
    first = (1 - side_ref[0]) * features + core_ref[0] * part
    sources = (q_hbm, grads_hbm, error_hbm.at[pl.ds(pl.multiple_of(first, part), part)], pair_hbm)
    targets = (q_ref, grads_ref, error_ref.at[0], error_ref.at[1])
    copies = [
        pltpu.make_async_copy(source, target, arrived.at[i])
        for i, (source, target) in enumerate(zip(sources, targets))
    ]
    for copy in copies:
        copy.start()
    copies[0].wait()
    q_parts = split(q_ref[...], 0)
    copies[1].wait()
    payload_ref[:, part:] = times_q(q_parts, grads_ref[...]).astype(BF16)
    copies[2].wait()
    copies[3].wait()
    for start in range(0, part, STEP):
        rows = slice(start, start + STEP)
        total = times_q(q_parts, error_ref[0, rows]) + times_q(q_parts, error_ref[1, rows])
        payload_ref[:, rows] = total.astype(BF16)


def project(side, core, q_prev, grads, error, error_pair):
    rank, columns = q_prev.shape
    tokens, part = grads.shape[0], error_pair.shape[0]
    smem = pl.BlockSpec(memory_space=pltpu.SMEM)
    hbm = pl.BlockSpec(memory_space=pltpu.HBM)
    return pl.pallas_call(
        project_kernel,
        out_shape=jax.ShapeDtypeStruct((rank, part + tokens), BF16),
        in_specs=[smem, smem, hbm, hbm, hbm, hbm],
        out_specs=pl.BlockSpec(memory_space=pltpu.VMEM),
        scratch_shapes=[
            pltpu.VMEM((rank, columns), F32),
            pltpu.VMEM((tokens, columns), BF16),
            pltpu.VMEM((2, part, columns), BF16),
            pltpu.SemaphoreType.DMA((4,)),
        ],
        cost_estimate=pl.CostEstimate(flops=10**8, bytes_accessed=2 * 10**6, transcendentals=0),
        compiler_params=pltpu.CompilerParams(vmem_limit_bytes=VMEM_ALL),
        name="project",
    )(side, core, q_prev, grads, error, error_pair)


def left_kernel(groups, side_ref, core_ref, pair_ref, q_ref, error_ref, inputs_ref, out_ref):
    features, side = inputs_ref.shape[1], side_ref[0]
    rank = q_ref.shape[0]
    payload_ref, near_ref = pair_ref.at[side], pair_ref.at[1 - side]
    q_parts = split(q_ref[...], 0)
    part = payload_ref.shape[1] - inputs_ref.shape[0]
    mixed = jnp.concatenate([payload_ref[:, part:], near_ref[:, part:]], axis=0)
    for start in range(0, features, STEP):
        lanes = slice(start, start + STEP)
        rows = pl.ds(pl.multiple_of(side * features + start, STEP), STEP)
        product = dot(mixed, inputs_ref[:, lanes])
        own = (product[:rank] + times_q(q_parts, error_ref[rows])) * (1.0 / groups)
        carried = near_ref[:, start % part : start % part + STEP].astype(F32)
        carried = jnp.where(core_ref[0] == start // part, carried, 0.0)
        near = (product[rank:] + carried) * (1.0 / groups)
        out_ref[0, :, lanes] = own.astype(BF16)
        out_ref[1, :, lanes] = near.astype(BF16)


def chip_sum_kernel(pair_ref, out_ref):
    chunks, _, width = out_ref.shape
    for chunk in range(chunks):
        lanes = slice(chunk * width, (chunk + 1) * width)
        total = pair_ref[0, :, lanes].astype(F32) + pair_ref[1, :, lanes].astype(F32)
        out_ref[chunk] = total.astype(BF16)


def share_kernel(shares_ref, out_ref):
    groups, rank, _ = shares_ref.shape
    for core in range(2):
        total = shares_ref[core].astype(F32)
        for member in range(core + 2, groups, 2):
            total += shares_ref[member].astype(F32)
        out_ref[core * rank : (core + 1) * rank] = total.astype(BF16)


def two_chunks(factor_ref, chunk, rows):
    return jnp.concatenate([factor_ref[chunk, rows], factor_ref[chunk + 1, rows]], axis=1)


def right_kernel(core_ref, factor_ref, inputs_ref, away_ref, projected_ref, gram_ref):
    chunks, both, width = factor_ref.shape
    rank, half = both // 2, chunks // 2
    tokens = inputs_ref.shape[0]
    projected = jnp.zeros((both, tokens), F32)
    gram = jnp.zeros((both, both), F32)
    for chunk in range(0, chunks, 2):
        factor = two_chunks(factor_ref, chunk, slice(None))
        projected += dot(factor, inputs_ref[:, chunk * width : (chunk + 2) * width], 1, 1)
        gram += dot(factor, factor, 1, 1)
    for chunk in range(half):
        lanes = slice(chunk * width, (chunk + 1) * width)
        away_ref[:, lanes] = factor_ref[core_ref[0] * half + chunk, rank:]
    start = half * width
    away_ref[:, start : start + tokens] = projected[rank:].astype(BF16)
    away_ref[:, start + tokens :] = split(gram[rank:, rank:], 1)
    projected_ref[...] = projected[:rank]
    gram_ref[...] = gram[:rank, :rank]


def join_kernel(
    side_ref, core_ref, pair_ref, factor_ref, projected_ref, grads_ref, error_ref, error_pair_ref,
    out_ref,
):
    chunks, both, width = factor_ref.shape
    rank, tokens = both // 2, grads_ref.shape[0]
    features, part = chunks * width, error_pair_ref.shape[0]
    side = side_ref[0]
    near_ref = pair_ref.at[1 - side]
    near = near_ref[:, part : part + tokens].astype(F32)
    total = dot((projected_ref[...] + near).astype(BF16), grads_ref[...])
    size = 2 * width
    for start in range(0, features, size):
        rows = pl.ds(pl.multiple_of(side * features + start, size), size)
        total += dot(two_chunks(factor_ref, start // width, slice(rank)), error_ref[rows])
    for start in range(0, part, size):
        lanes = slice(start, start + size)
        first = (1 - side) * features + core_ref[0] * part + start
        rows = pl.ds(pl.multiple_of(first, size), size)
        total += dot(near_ref[:, lanes], error_ref[rows])
        total += dot(near_ref[:, lanes], error_pair_ref[lanes])
    out_ref[...] = total.astype(BF16)


def spread_kernel(core_ref, pair_ref, out_ref):
    copies, _, width = out_ref.shape
    lanes = pl.ds(pl.multiple_of(core_ref[0] * width, width), width)
    total = pair_ref[0, :, lanes].astype(F32) + pair_ref[1, :, lanes].astype(F32)
    total = total.astype(BF16)
    for copy in range(copies):
        out_ref[copy] = total


def invert_kernel(side_ref, pair_ref, own_ref, out_ref):
    rank = out_ref.shape[0]
    start = pair_ref.shape[2] - 2 * rank
    near = pair_ref[1 - side_ref[0], :, start:].astype(F32)
    gram = own_ref[...] + near[:, :rank] + near[:, rank:]
    rows = lax.broadcasted_iota(jnp.int32, (rank, 2 * rank), 0)
    lanes = lax.broadcasted_iota(jnp.int32, (rank, 2 * rank), 1)
    identity = (lanes - rank == rows).astype(F32)
    work = jnp.concatenate([gram, gram], axis=1)
    work = jnp.where(lanes < rank, work, identity)
    for start in range(0, rank, WIDE):
        top = start // 8 * 8
        active = work[top:]
        columns = [
            jnp.broadcast_to(active[:, start + i : start + i + 1], active.shape)
            for i in range(WIDE)
        ]
        for i in range(WIDE):
            row = start + i - top
            scale = 1.0 / columns[i][row : row + 1]
            below = jnp.where(rows[top:] > start + i, columns[i], 0.0)
            for j in range(i + 1, WIDE):
                across = columns[i][row + j - i : row + j - i + 1] * scale
                columns[j] = columns[j] - below * across
            active = active - below * (active[row : row + 1] * scale)
        work = active if top == 0 else jnp.concatenate([work[:top], active], axis=0)
    diagonal = jnp.sum(jnp.where(lanes == rows, work, 0.0), axis=1, keepdims=True)
    out_ref[...] = (work * lax.rsqrt(diagonal))[:, rank:]


def finish_kernel(gathered_ref, inverse_ref, out_ref):
    members, _, width = gathered_ref.shape
    cores = out_ref.shape[1] // width
    for core in range(cores):
        total = gathered_ref[core].astype(F32)
        for member in range(core + cores, members, cores):
            total += gathered_ref[member].astype(F32)
        out_ref[:, core * width : (core + 1) * width] = jnp.dot(
            inverse_ref[...], total * (1.0 / members), precision=HIGHEST, preferred_element_type=F32
        )


def input_grad_kernel(side_ref, grads_ref, grads_near_ref, weight_ref, out_ref):
    step, side = pl.program_id(0), side_ref[0]
    half = weight_ref.shape[0] // 2
    own = weight_ref[(1 - side) * half + half - 1 - step]
    near = weight_ref[side * half + step]
    total = dot(grads_ref[...], own, 1, 1) + dot(grads_near_ref[...], near, 1, 1)
    out_ref[...] = total.astype(BF16)


def input_grad(side, grads, grads_near, weight):
    tokens, _ = grads.shape
    pieces, rows, _ = weight.shape
    vmem = pl.BlockSpec(memory_space=pltpu.VMEM)
    return pl.pallas_call(
        input_grad_kernel,
        out_shape=jax.ShapeDtypeStruct((tokens, pieces // 2 * rows), BF16),
        grid=(pieces // 2,),
        in_specs=[pl.BlockSpec(memory_space=pltpu.SMEM), vmem, vmem, vmem],
        out_specs=pl.BlockSpec((tokens, rows), lambda step: (0, step)),
        cost_estimate=pl.CostEstimate(flops=10**9, bytes_accessed=3 * 10**6, transcendentals=0),
        compiler_params=pltpu.CompilerParams(vmem_limit_bytes=VMEM_LIMIT),
        name="input_grad",
    )(side, grads, grads_near, weight)


def weight_route(chips, cores, sections):
    def index(z, c, s, t):
        return ((z * cores + c) * sections + s) * 2 + t

    route = []
    for s in range(sections - 1):
        for z in range(chips):
            for c in range(cores):
                for t in range(2):
                    if z // (chips // 2) == t:
                        source = index(z, c, s + 1, 1 - t)
                    else:
                        source = index(chips - 1 - z, c, s + 1, t)
                    route.append((source, index(z, c, s, t)))
    return route


def on_device(activations, key_grads, key_weight, error_buf, q_prev):
    chips, cores, sections = (lax.axis_size(name) for name in ("z", "c", "pp"))
    groups = chips * cores
    side, core = place("tp"), place("c")
    inputs, grads, weight, error = activations[0], key_grads[0], key_weight[0], error_buf[0, 0]
    rank = q_prev.shape[2]
    tokens, features = inputs.shape
    columns = grads.shape[1]
    part = features // groups

    def shape(*sizes, kind=F32):
        return jax.ShapeDtypeStruct(sizes, kind)

    weight_piece = lax.ppermute(
        weight, ("z", "c", "pp", "tp"), weight_route(chips, cores, sections)
    )

    error_part = features // cores
    error_away = (1 - side[0]) * features + (1 - core[0]) * error_part
    error_pair = swap(lax.dynamic_slice_in_dim(error, error_away, error_part, 0), "c")

    q_rows = q_prev[0].T
    payload = project(side, core, q_rows, grads, error, error_pair)
    payload = lax.all_gather(payload, "tp", axis=0, tiled=False)
    payload, weight_piece = lax.optimization_barrier((payload, weight_piece))
    weight_all = lax.all_gather(weight_piece, GROUP, axis=0, tiled=False)
    factor = call(
        lambda *refs: left_kernel(groups, *refs),
        shape(cores, rank, features, kind=BF16),
        "left",
        (side, core, payload, q_rows, error, inputs),
        scalars=2,
    )
    factor = lax.all_to_all(factor, "c", 0, 0)
    shares = call(
        chip_sum_kernel,
        shape(groups, rank, part, kind=BF16),
        "chip_sum",
        (factor,),
        scalars=0,
    )
    shares, grads_later = lax.optimization_barrier((shares, grads))
    shares = lax.all_to_all(shares, GROUP, 0, 0)
    grads_next = lax.ppermute(grads_later, "pp", [(i, i - 1) for i in range(1, sections)])
    grads_next_near = lax.ppermute(
        grads_later,
        ("pp", "tp"),
        [(2 * s + 2 + 1 - t, 2 * s + t) for s in range(sections - 1) for t in range(2)],
    )
    share = call(share_kernel, shape(2 * rank, part, kind=BF16), "share", (shares,), scalars=0)
    factor = lax.all_gather(share, GROUP, axis=0, tiled=False)
    factor, grads_next, grads_next_near = lax.optimization_barrier(
        (factor, grads_next, grads_next_near)
    )

    away, projected, gram = call(
        right_kernel,
        (
            shape(rank, error_part + tokens + 2 * rank, kind=BF16),
            shape(rank, tokens),
            shape(rank, rank),
        ),
        "right",
        (core, factor, inputs),
    )
    pair = lax.all_gather(away, "tp", axis=0, tiled=False)
    coeffs = call(
        join_kernel,
        shape(rank, columns, kind=BF16),
        "join",
        (side, core, pair, factor, projected, grads, error, error_pair),
        scalars=2,
    )
    coeffs = lax.all_gather(coeffs, "c", axis=0, tiled=False)
    spread = call(
        spread_kernel, shape(groups, rank, columns // cores, kind=BF16), "spread", (core, coeffs)
    )
    gathered = lax.all_to_all(spread, GROUP, 0, 0)
    inverse = call(invert_kernel, shape(rank, rank), "invert", (side, pair, gram))
    grad_prev = input_grad(
        side, grads_next, grads_next_near, weight_all.reshape(chips, cores * tokens, columns)
    )
    gathered, inverse, grad_prev = lax.optimization_barrier((gathered, inverse, grad_prev))
    coeffs = call(finish_kernel, shape(rank, columns), "finish", (gathered, inverse), scalars=0)
    return (grad_prev[None], coeffs.T[None])


def solution(mesh):
    groups, sections, sides = (mesh.shape[name] for name in ("dp", "pp", "tp"))
    split_mesh = Mesh(
        mesh.devices.reshape(groups // 2, 2, sections, sides), ("z", "c", "pp", "tp")
    )
    return jax.shard_map(
        on_device,
        mesh=split_mesh,
        in_specs=(
            P("pp", GROUP, "tp"),
            P("pp", GROUP, "tp"),
            P("pp", GROUP, "tp"),
            P("pp", GROUP, None, "tp"),
            P("pp", "tp", None),
        ),
        out_specs=(P("pp", GROUP, "tp"), P("pp", "tp", None)),
        check_vma=False,
    )
```

```python
import jax
import jax.numpy as jnp
from jax import lax
from jax.experimental import pallas as pl
from jax.experimental.pallas import tpu as pltpu
from jax.sharding import Mesh
from jax.sharding import PartitionSpec as P

HIGHEST = lax.Precision.HIGHEST
BF16 = jnp.bfloat16
F32 = jnp.float32
GROUP = ("z", "c")
VMEM_LIMIT = 12 * 2**20
VMEM_ALL = 60 * 2**20
STEP = 512
WIDE = 4


def swap(block, axis):
    return lax.ppermute(block, axis, [(0, 1), (1, 0)])


def dot(a, b, a_dim=1, b_dim=0):
    return lax.dot_general(a, b, (((a_dim,), (b_dim,)), ((), ())), preferred_element_type=F32)


def split(values, axis):
    high = values.astype(BF16)
    return jnp.concatenate([high, (values - high.astype(F32)).astype(BF16)], axis=axis)


def place(name):
    return lax.axis_index(name).astype(jnp.int32).reshape(1)


def call(kernel, out_shapes, name, operands, scalars=1, flops=10**8, moved=4 * 10**6):
    spaces = [pltpu.SMEM] * scalars + [pltpu.VMEM] * (len(operands) - scalars)
    return pl.pallas_call(
        kernel,
        out_shape=out_shapes,
        in_specs=[pl.BlockSpec(memory_space=space) for space in spaces],
        cost_estimate=pl.CostEstimate(flops=flops, bytes_accessed=moved, transcendentals=0),
        compiler_params=pltpu.CompilerParams(vmem_limit_bytes=VMEM_LIMIT),
        name=name,
    )(*operands)


def times_q(q_parts, block):
    rank = q_parts.shape[0] // 2
    both = dot(q_parts, block, 1, 1)
    return both[:rank] + both[rank:]


def project_kernel(
    side_ref, core_ref, q_hbm, grads_hbm, error_hbm, pair_hbm, payload_ref,
    q_ref, grads_ref, error_ref, arrived,
):
    part = pair_hbm.shape[0]
    features = error_hbm.shape[0] // 2
    first = (1 - side_ref[0]) * features + core_ref[0] * part
    sources = (q_hbm, grads_hbm, error_hbm.at[pl.ds(pl.multiple_of(first, part), part)], pair_hbm)
    targets = (q_ref, grads_ref, error_ref.at[0], error_ref.at[1])
    copies = [
        pltpu.make_async_copy(source, target, arrived.at[i])
        for i, (source, target) in enumerate(zip(sources, targets))
    ]
    for copy in copies:
        copy.start()
    copies[0].wait()
    q_parts = split(q_ref[...], 0)
    copies[1].wait()
    payload_ref[:, part:] = times_q(q_parts, grads_ref[...]).astype(BF16)
    copies[2].wait()
    copies[3].wait()
    for start in range(0, part, STEP):
        rows = slice(start, start + STEP)
        total = times_q(q_parts, error_ref[0, rows]) + times_q(q_parts, error_ref[1, rows])
        payload_ref[:, rows] = total.astype(BF16)


def project(side, core, q_prev, grads, error, error_pair):
    rank, columns = q_prev.shape
    tokens, part = grads.shape[0], error_pair.shape[0]
    smem = pl.BlockSpec(memory_space=pltpu.SMEM)
    hbm = pl.BlockSpec(memory_space=pltpu.HBM)
    return pl.pallas_call(
        project_kernel,
        out_shape=jax.ShapeDtypeStruct((rank, part + tokens), BF16),
        in_specs=[smem, smem, hbm, hbm, hbm, pl.BlockSpec(memory_space=pl.ANY)],
        out_specs=pl.BlockSpec(memory_space=pltpu.VMEM),
        scratch_shapes=[
            pltpu.VMEM((rank, columns), F32),
            pltpu.VMEM((tokens, columns), BF16),
            pltpu.VMEM((2, part, columns), BF16),
            pltpu.SemaphoreType.DMA((4,)),
        ],
        cost_estimate=pl.CostEstimate(flops=10**8, bytes_accessed=2 * 10**6, transcendentals=0),
        compiler_params=pltpu.CompilerParams(vmem_limit_bytes=VMEM_ALL),
        name="project",
    )(side, core, q_prev, grads, error, error_pair)


def left_kernel(groups, side_ref, core_ref, pair_ref, q_ref, error_ref, inputs_ref, out_ref):
    features, side = inputs_ref.shape[1], side_ref[0]
    rank = q_ref.shape[0]
    payload_ref, near_ref = pair_ref.at[side], pair_ref.at[1 - side]
    q_parts = split(q_ref[...], 0)
    part = payload_ref.shape[1] - inputs_ref.shape[0]
    mixed = jnp.concatenate([payload_ref[:, part:], near_ref[:, part:]], axis=0)
    for start in range(0, features, STEP):
        lanes = slice(start, start + STEP)
        rows = pl.ds(pl.multiple_of(side * features + start, STEP), STEP)
        product = dot(mixed, inputs_ref[:, lanes])
        own = (product[:rank] + times_q(q_parts, error_ref[rows])) * (1.0 / groups)
        carried = near_ref[:, start % part : start % part + STEP].astype(F32)
        carried = jnp.where(core_ref[0] == start // part, carried, 0.0)
        near = (product[rank:] + carried) * (1.0 / groups)
        out_ref[0, :, lanes] = own.astype(BF16)
        out_ref[1, :, lanes] = near.astype(BF16)


def chip_sum_kernel(pair_ref, out_ref):
    chunks, _, width = out_ref.shape
    for chunk in range(chunks):
        lanes = slice(chunk * width, (chunk + 1) * width)
        total = pair_ref[0, :, lanes].astype(F32) + pair_ref[1, :, lanes].astype(F32)
        out_ref[chunk] = total.astype(BF16)


def share_kernel(shares_ref, out_ref):
    groups, rank, _ = shares_ref.shape
    for core in range(2):
        total = shares_ref[core].astype(F32)
        for member in range(core + 2, groups, 2):
            total += shares_ref[member].astype(F32)
        out_ref[core * rank : (core + 1) * rank] = total.astype(BF16)


def two_chunks(factor_ref, chunk, rows):
    return jnp.concatenate([factor_ref[chunk, rows], factor_ref[chunk + 1, rows]], axis=1)


def right_kernel(core_ref, factor_ref, inputs_ref, away_ref, projected_ref, gram_ref):
    chunks, both, width = factor_ref.shape
    rank, half = both // 2, chunks // 2
    tokens = inputs_ref.shape[0]
    projected = jnp.zeros((both, tokens), F32)
    gram = jnp.zeros((both, both), F32)
    for chunk in range(0, chunks, 2):
        factor = two_chunks(factor_ref, chunk, slice(None))
        projected += dot(factor, inputs_ref[:, chunk * width : (chunk + 2) * width], 1, 1)
        gram += dot(factor, factor, 1, 1)
    for chunk in range(half):
        lanes = slice(chunk * width, (chunk + 1) * width)
        away_ref[:, lanes] = factor_ref[core_ref[0] * half + chunk, rank:]
    start = half * width
    away_ref[:, start : start + tokens] = projected[rank:].astype(BF16)
    away_ref[:, start + tokens :] = split(gram[rank:, rank:], 1)
    projected_ref[...] = projected[:rank]
    gram_ref[...] = gram[:rank, :rank]


def join_kernel(
    side_ref, core_ref, pair_ref, factor_ref, projected_ref, grads_ref, error_ref, error_pair_ref,
    out_ref,
):
    chunks, both, width = factor_ref.shape
    rank, tokens = both // 2, grads_ref.shape[0]
    features, part = chunks * width, error_pair_ref.shape[0]
    side = side_ref[0]
    near_ref = pair_ref.at[1 - side]
    near = near_ref[:, part : part + tokens].astype(F32)
    total = dot((projected_ref[...] + near).astype(BF16), grads_ref[...])
    size = 2 * width
    for start in range(0, features, size):
        rows = pl.ds(pl.multiple_of(side * features + start, size), size)
        total += dot(two_chunks(factor_ref, start // width, slice(rank)), error_ref[rows])
    for start in range(0, part, size):
        lanes = slice(start, start + size)
        first = (1 - side) * features + core_ref[0] * part + start
        rows = pl.ds(pl.multiple_of(first, size), size)
        total += dot(near_ref[:, lanes], error_ref[rows])
        total += dot(near_ref[:, lanes], error_pair_ref[lanes])
    out_ref[...] = total.astype(BF16)


def spread_kernel(core_ref, pair_ref, out_ref):
    copies, _, width = out_ref.shape
    lanes = pl.ds(pl.multiple_of(core_ref[0] * width, width), width)
    total = pair_ref[0, :, lanes].astype(F32) + pair_ref[1, :, lanes].astype(F32)
    total = total.astype(BF16)
    for copy in range(copies):
        out_ref[copy] = total


def invert_kernel(side_ref, pair_ref, own_ref, out_ref):
    rank = out_ref.shape[0]
    start = pair_ref.shape[2] - 2 * rank
    near = pair_ref[1 - side_ref[0], :, start:].astype(F32)
    gram = own_ref[...] + near[:, :rank] + near[:, rank:]
    rows = lax.broadcasted_iota(jnp.int32, (rank, 2 * rank), 0)
    lanes = lax.broadcasted_iota(jnp.int32, (rank, 2 * rank), 1)
    identity = (lanes - rank == rows).astype(F32)
    work = jnp.concatenate([gram, gram], axis=1)
    work = jnp.where(lanes < rank, work, identity)
    for start in range(0, rank, WIDE):
        top = start // 8 * 8
        active = work[top:]
        columns = [
            jnp.broadcast_to(active[:, start + i : start + i + 1], active.shape)
            for i in range(WIDE)
        ]
        for i in range(WIDE):
            row = start + i - top
            scale = 1.0 / columns[i][row : row + 1]
            below = jnp.where(rows[top:] > start + i, columns[i], 0.0)
            for j in range(i + 1, WIDE):
                across = columns[i][row + j - i : row + j - i + 1] * scale
                columns[j] = columns[j] - below * across
            active = active - below * (active[row : row + 1] * scale)
        work = active if top == 0 else jnp.concatenate([work[:top], active], axis=0)
    diagonal = jnp.sum(jnp.where(lanes == rows, work, 0.0), axis=1, keepdims=True)
    out_ref[...] = (work * lax.rsqrt(diagonal))[:, rank:]


def finish_kernel(gathered_ref, inverse_ref, out_ref):
    members, _, width = gathered_ref.shape
    cores = out_ref.shape[1] // width
    for core in range(cores):
        total = gathered_ref[core].astype(F32)
        for member in range(core + cores, members, cores):
            total += gathered_ref[member].astype(F32)
        out_ref[:, core * width : (core + 1) * width] = jnp.dot(
            inverse_ref[...], total * (1.0 / members), precision=HIGHEST, preferred_element_type=F32
        )


def input_grad_kernel(side_ref, grads_ref, grads_near_ref, weight_ref, out_ref):
    step, side = pl.program_id(0), side_ref[0]
    half = weight_ref.shape[0] // 2
    own = weight_ref[(1 - side) * half + half - 1 - step]
    near = weight_ref[side * half + step]
    total = dot(grads_ref[...], own, 1, 1) + dot(grads_near_ref[...], near, 1, 1)
    out_ref[...] = total.astype(BF16)


def input_grad(side, grads, grads_near, weight):
    tokens, _ = grads.shape
    pieces, rows, _ = weight.shape
    vmem = pl.BlockSpec(memory_space=pltpu.VMEM)
    return pl.pallas_call(
        input_grad_kernel,
        out_shape=jax.ShapeDtypeStruct((tokens, pieces // 2 * rows), BF16),
        grid=(pieces // 2,),
        in_specs=[pl.BlockSpec(memory_space=pltpu.SMEM), vmem, vmem, vmem],
        out_specs=pl.BlockSpec((tokens, rows), lambda step: (0, step)),
        cost_estimate=pl.CostEstimate(flops=10**9, bytes_accessed=3 * 10**6, transcendentals=0),
        compiler_params=pltpu.CompilerParams(vmem_limit_bytes=VMEM_LIMIT),
        name="input_grad",
    )(side, grads, grads_near, weight)


def weight_route(chips, cores, sections):
    def index(z, c, s, t):
        return ((z * cores + c) * sections + s) * 2 + t

    route = []
    for s in range(sections - 1):
        for z in range(chips):
            for c in range(cores):
                for t in range(2):
                    if z // (chips // 2) == t:
                        source = index(z, c, s + 1, 1 - t)
                    else:
                        source = index(chips - 1 - z, c, s + 1, t)
                    route.append((source, index(z, c, s, t)))
    return route


def on_device(activations, key_grads, key_weight, error_buf, q_prev):
    chips, cores, sections = (lax.axis_size(name) for name in ("z", "c", "pp"))
    groups = chips * cores
    side, core = place("tp"), place("c")
    inputs, grads, weight, error = activations[0], key_grads[0], key_weight[0], error_buf[0, 0]
    rank = q_prev.shape[2]
    tokens, features = inputs.shape
    columns = grads.shape[1]
    part = features // groups

    def shape(*sizes, kind=F32):
        return jax.ShapeDtypeStruct(sizes, kind)

    weight_piece = lax.ppermute(
        weight, ("z", "c", "pp", "tp"), weight_route(chips, cores, sections)
    )

    error_part = features // cores
    error_away = (1 - side[0]) * features + (1 - core[0]) * error_part
    error_pair = swap(lax.dynamic_slice_in_dim(error, error_away, error_part, 0), "c")

    q_rows = q_prev[0].T
    payload = project(side, core, q_rows, grads, error, error_pair)
    payload = lax.all_gather(payload, "tp", axis=0, tiled=False)
    payload, weight_piece = lax.optimization_barrier((payload, weight_piece))
    weight_all = lax.all_gather(weight_piece, GROUP, axis=0, tiled=False)
    factor = call(
        lambda *refs: left_kernel(groups, *refs),
        shape(cores, rank, features, kind=BF16),
        "left",
        (side, core, payload, q_rows, error, inputs),
        scalars=2,
    )
    factor = lax.all_to_all(factor, "c", 0, 0)
    shares = call(
        chip_sum_kernel,
        shape(groups, rank, part, kind=BF16),
        "chip_sum",
        (factor,),
        scalars=0,
    )
    shares, grads_later = lax.optimization_barrier((shares, grads))
    shares = lax.all_to_all(shares, GROUP, 0, 0)
    grads_next = lax.ppermute(grads_later, "pp", [(i, i - 1) for i in range(1, sections)])
    grads_next_near = lax.ppermute(
        grads_later,
        ("pp", "tp"),
        [(2 * s + 2 + 1 - t, 2 * s + t) for s in range(sections - 1) for t in range(2)],
    )
    share = call(share_kernel, shape(2 * rank, part, kind=BF16), "share", (shares,), scalars=0)
    factor = lax.all_gather(share, GROUP, axis=0, tiled=False)
    factor, grads_next, grads_next_near = lax.optimization_barrier(
        (factor, grads_next, grads_next_near)
    )

    away, projected, gram = call(
        right_kernel,
        (
            shape(rank, error_part + tokens + 2 * rank, kind=BF16),
            shape(rank, tokens),
            shape(rank, rank),
        ),
        "right",
        (core, factor, inputs),
    )
    pair = lax.all_gather(away, "tp", axis=0, tiled=False)
    coeffs = call(
        join_kernel,
        shape(rank, columns, kind=BF16),
        "join",
        (side, core, pair, factor, projected, grads, error, error_pair),
        scalars=2,
    )
    coeffs = lax.all_gather(coeffs, "c", axis=0, tiled=False)
    spread = call(
        spread_kernel, shape(groups, rank, columns // cores, kind=BF16), "spread", (core, coeffs)
    )
    gathered = lax.all_to_all(spread, GROUP, 0, 0)
    inverse = call(invert_kernel, shape(rank, rank), "invert", (side, pair, gram))
    grad_prev = input_grad(
        side, grads_next, grads_next_near, weight_all.reshape(chips, cores * tokens, columns)
    )
    gathered, inverse, grad_prev = lax.optimization_barrier((gathered, inverse, grad_prev))
    coeffs = call(finish_kernel, shape(rank, columns), "finish", (gathered, inverse), scalars=0)
    return (grad_prev[None], coeffs.T[None])


def solution(mesh):
    groups, sections, sides = (mesh.shape[name] for name in ("dp", "pp", "tp"))
    split_mesh = Mesh(
        mesh.devices.reshape(groups // 2, 2, sections, sides), ("z", "c", "pp", "tp")
    )
    return jax.shard_map(
        on_device,
        mesh=split_mesh,
        in_specs=(
            P("pp", GROUP, "tp"),
            P("pp", GROUP, "tp"),
            P("pp", GROUP, "tp"),
            P("pp", GROUP, None, "tp"),
            P("pp", "tp", None),
        ),
        out_specs=(P("pp", GROUP, "tp"), P("pp", "tp", None)),
        check_vma=False,
    )
```
